32 devices in a mesh: grp: 2 (over x), state: 16 (over z, y, core).
Axes of the slice: x: 2, y: 2, z: 4, core: 2. Of those that a mesh axis runs over, the one named last changes fastest.
Arguments:
- prior_mean: bfloat16 [131072], P(('grp', 'state')), parts along dimension 0, may hold values from -6 to 6
- prior_root: bfloat16 [131072, 512], P(('grp', 'state')), parts along dimension 0, may hold values from -11.2 to 11.2
- process_noise_factor: bfloat16 [131072, 128], P(('grp', 'state')), parts along dimension 0, may hold values from -3 to 3
- tangent_operator_tiles: bfloat16 [1024, 3, 128, 128], P(('grp', 'state')), parts along dimension 0, may hold values from -0.3125 to 0.3125
- tile_target_placing: int32 [1024, 3], P(('grp', 'state')), parts along dimension 0, may hold values from 0 to 511, as said below
- start_basis: int32 [640, 512], replicated, may hold values from -4 to 4
- obs_cell: int32 [1024, 16], P(('grp', 'state')), parts along dimension 0, may hold values from 0 to 127
- measured_surge_levels: float32 [1024, 16], P(('grp', 'state')), parts along dimension 0, may hold values from -8 to 8
- obs_precision: float32 [1024, 16], P(('grp', 'state')), parts along dimension 0, may hold values from 6.1035156e-05 to 0.0009765625
Outputs:
- posterior_average: float32 [131072], P(('grp', 'state')), parts along dimension 0
- posterior_root: bfloat16 [131072, 512], P(('grp', 'state')), parts along dimension 0
The draws below stay inside these ranges and needn't reach their ends.
There are 2 independent parts, one for each index of `grp`. The reference program is written for one: setup_inputs(seed, part) draws one part's arguments, and reference() takes and returns one part's arrays. A program takes and returns all parts, laid end to end along the dimension named above; an argument that names none is the same for every part. Nothing has to cross between parts.
Inputs may be any that keep to these rules, and one draw needn't show every extreme that they name: `tile_target_placing`: column 0 of row b is b itself; column 1 lies 1 to 2 blocks below b and column 2 lies 1 to 2 blocks above b, both clipped to the grid's blocks.
All inputs are finite; a program needn't handle non-finite values.
Results may differ from the reference program's by a relative error of at most 0.0095.
Values may be sent and summed in bfloat16 or wider, within the bound.
No kernel may reach another device: no remote copies, remote signals or barrier semaphores. Data moves between devices by JAX's collectives and lax.ppermute only.
A program may use at most 128 MiB of HBM per device.

```python
import math
import jax
import jax.numpy as jnp
from jax import lax

BS = 128
SPAN = 2
FACTOR_RANK = 512
NOISE = 128
ITERS = 2
NOBS = 16
COLS = 640
NBLOCKS = 512
GRID_POINTS = 65536


def draw_tile_target_placing(key, part):
    key = jax.random.fold_in(key, 7)
    lower_key, upper_key = jax.random.split(key)
    diagonal_index = jnp.arange(NBLOCKS, dtype=jnp.int32)
    below_index = jnp.clip(diagonal_index - jax.random.randint(lower_key, (NBLOCKS,), 1, SPAN + 1), 0, NBLOCKS - 1)
    above_index = jnp.clip(diagonal_index + jax.random.randint(upper_key, (NBLOCKS,), 1, SPAN + 1), 0, NBLOCKS - 1)
    return jnp.stack([diagonal_index, below_index, above_index], axis=1).astype(jnp.int32)


def draw_prior_root(key, part):
    key = jax.random.fold_in(key, 11)
    base_key, column_key, row_key = jax.random.split(key, 3)
    column_scale = jnp.exp(jax.random.uniform(column_key, (FACTOR_RANK,), jnp.float32, math.log(0.6), math.log(2.0)))
    row_scale = jnp.exp(jax.random.uniform(row_key, (GRID_POINTS, 1), jnp.float32, math.log(0.7), math.log(1.4)))
    base = jnp.clip(jax.random.normal(base_key, (GRID_POINTS, FACTOR_RANK), jnp.float32), -4.0, 4.0)
    return (base * row_scale * column_scale).astype(jnp.bfloat16)


def set_ends(drawn, stream_key, low, top_value):
    spot = [jax.random.randint(jax.random.fold_in(stream_key, axis), (), 0, length) for axis, length in enumerate(drawn.shape)]
    longest = drawn.shape.index(max(drawn.shape))
    next_to = spot[:longest] + [(spot[longest] + 1) % drawn.shape[longest]] + spot[longest + 1:]
    return drawn.at[tuple(spot)].set(low).at[tuple(next_to)].set(top_value)


def steps_of(key, shape, shards, smallest, high):
    def one(axis_at, parts):
        steps = jax.random.uniform(jax.random.fold_in(jax.random.fold_in(key, 6), axis_at), (parts,), jnp.float32, smallest / len(shards), high / len(shards))
        return jnp.repeat(jnp.exp(steps), shape[axis_at] // parts).reshape((-1,) + (1,) * (len(shape) - axis_at - 1))

    level = one(*shards[0])
    for cut in shards[1:]:
        level = level * one(*cut)
    return level


def gaussian(key, dims, spread, limit, shards=(), kind=jnp.bfloat16):
    entries = spread * jax.random.normal(key, dims, jnp.float32)
    if shards:
        entries = entries * steps_of(key, dims, shards, -0.22, 0.18)
    return jnp.clip(entries, -limit, limit).astype(kind)


def setup_inputs(seed: int = 0, part: int = 0) -> dict:
    keys = jax.random.split(jax.random.key(seed), 10)
    part_splits = jax.random.split(jax.random.fold_in(keys[9], part), 10)
    return {
        "prior_mean": gaussian(part_splits[0], (GRID_POINTS,), 1.0, 6.0, ((0, 16),)),
        "prior_root": draw_prior_root(jax.random.fold_in(jax.random.fold_in(keys[9], part), 71), part),
        "process_noise_factor": gaussian(part_splits[2], (GRID_POINTS, NOISE), 0.5, 3.0, ((0, 16),)),
        "tangent_operator_tiles": gaussian(part_splits[3], (NBLOCKS, 3, BS, BS), (3 * BS) ** -0.5, 0.3125, ((0, 16),)),
        "tile_target_placing": draw_tile_target_placing(jax.random.fold_in(jax.random.fold_in(keys[9], part), 71), part),
        "start_basis": set_ends(jax.random.randint(keys[5], (COLS, FACTOR_RANK), -4, 5), jax.random.fold_in(keys[5], 1), -4, 4).astype(jnp.int32),
        "obs_cell": set_ends(jax.random.randint(part_splits[6], (NBLOCKS, NOBS), 0, BS), jax.random.fold_in(part_splits[6], 1), 0, BS - 1).astype(jnp.int32),
        "measured_surge_levels": gaussian(part_splits[7], (NBLOCKS, NOBS), 1.5, 8.0, ((0, 16),), jnp.float32),
        "obs_precision": jnp.clip(jnp.exp(math.log(0.0009765625) - 2.7725887 * jax.random.uniform(part_splits[8], (NBLOCKS, NOBS), jnp.float32) ** steps_of(part_splits[8], (NBLOCKS, NOBS), ((0, 16),), -0.2, 0.2)), 6.103515625e-05, 0.0009765625),
    }


def propagate_step(tangent_operator_tiles, tile_target_placing, field):
    total = jnp.zeros(field.shape, jnp.float32)
    for member in range(3):
        picked = field[tile_target_placing[:, member]]
        total = total + jnp.einsum('bij,bjr->bir', tangent_operator_tiles[:, member].astype(jnp.float32), picked)
    return total

def reference(prior_mean, prior_root, process_noise_factor, tangent_operator_tiles, tile_target_placing, start_basis, obs_cell, measured_surge_levels, obs_precision):
    tile_factors = prior_root.astype(jnp.float32).reshape(NBLOCKS, BS, FACTOR_RANK)
    tile_averages = prior_mean.astype(jnp.float32).reshape(NBLOCKS, BS, 1)
    predicted_factor = propagate_step(tangent_operator_tiles, tile_target_placing, tile_factors).reshape(GRID_POINTS, FACTOR_RANK).astype(jnp.bfloat16)
    predicted_average = propagate_step(tangent_operator_tiles, tile_target_placing, tile_averages).reshape(GRID_POINTS)
    stacked_factor_matrix = jnp.concatenate([predicted_factor, process_noise_factor], axis=1)
    gram = jnp.dot(stacked_factor_matrix.T.astype(jnp.float32), stacked_factor_matrix.astype(jnp.float32), preferred_element_type=jnp.float32)
    basis = start_basis.astype(jnp.float32)
    for sweep in range(ITERS):
        image = jnp.dot(gram, basis, precision=lax.Precision.HIGHEST)
        inner = jnp.dot(image.T, image, precision=lax.Precision.HIGHEST)
        lower = jnp.linalg.cholesky(inner)
        basis = lax.linalg.triangular_solve(lower, image, left_side=False, lower=True, transpose_a=True)
    adjusted_surge_vector = jnp.dot(stacked_factor_matrix.astype(jnp.float32), basis.astype(jnp.bfloat16).astype(jnp.float32), preferred_element_type=jnp.float32).astype(jnp.bfloat16)
    gauge_positions = (jnp.arange(NBLOCKS, dtype=jnp.int32)[:, None] * BS + obs_cell).reshape(-1).astype(jnp.int32)
    observed = adjusted_surge_vector[gauge_positions].astype(jnp.float32)
    measurement_residual = measured_surge_levels.reshape(-1) - predicted_average[gauge_positions]
    weights = obs_precision.reshape(-1)
    info = jnp.dot(observed.T, weights[:, None] * observed, precision=lax.Precision.HIGHEST)
    pull = jnp.dot(observed.T, weights * measurement_residual, precision=lax.Precision.HIGHEST)
    identity = jnp.eye(FACTOR_RANK, dtype=jnp.float32)
    factor = jnp.linalg.cholesky(info + identity)
    inverse = lax.linalg.triangular_solve(factor, identity, left_side=True, lower=True)
    shift_magnitude = jnp.dot(inverse.T, jnp.dot(inverse, pull, precision=lax.Precision.HIGHEST), precision=lax.Precision.HIGHEST)
    extended_factor = adjusted_surge_vector.astype(jnp.float32)
    posterior_average = predicted_average + jnp.dot(extended_factor, shift_magnitude, precision=lax.Precision.HIGHEST)
    posterior_root = jnp.dot(extended_factor, inverse.T, precision=lax.Precision.HIGHEST).astype(jnp.bfloat16)
    return (posterior_average, posterior_root)
```

```python
import functools

import jax
import jax.numpy as jnp
from jax import lax
from jax.experimental import pallas as pl
from jax.experimental.pallas import tpu as pltpu
from jax.sharding import PartitionSpec as P

BS = 128
SPAN = 2
GROUP = 2
NB = 64
F32 = jnp.float32
BF16 = jnp.bfloat16
VMEM = pltpu.VMEM
LIMIT = pltpu.CompilerParams(vmem_limit_bytes=48 * 2**20)


def dot1(a, b, ca, cb):
    return lax.dot_general(a, b, (((ca,), (cb,)), ((), ())), preferred_element_type=F32)


def split(x):
    high = x.astype(BF16)
    return high, (x - high.astype(F32)).astype(BF16)


def dot3(a, b, ca, cb):
    return dot1(a[0], b[0], ca, cb) + (dot1(a[0], b[1], ca, cb) + dot1(a[1], b[0], ca, cb))


def pairs(count):
    return [(i, j) for i in range(count) for j in range(i, count)]


def forecast_step(step, index_ref, source, mean_source, tiles, noise, cell, level, weight):
    roots, means = [], []
    for k in range(GROUP):
        at = [index_ref[3 * (GROUP * step + k) + m] for m in range(3)]
        tile = jnp.concatenate([tiles[k, m] for m in range(3)], axis=1)
        picked = jnp.concatenate([source[a] for a in at], axis=0)
        roots.append(dot1(tile, picked, 1, 0).astype(BF16))
        mean = jnp.concatenate([mean_source[pl.ds(a, 1), :] for a in at], axis=1)
        mean = jnp.broadcast_to(mean, (16, 3 * BS)).astype(BF16)
        means.append(dot1(mean, tile, 1, 1)[0:1])
    stacked = jnp.concatenate([jnp.concatenate(roots, axis=0), noise[...]], axis=1)
    mean = jnp.concatenate(means, axis=1)
    rows = cell.shape[0]
    per = rows // GROUP
    shape = (rows, GROUP * BS)
    place = cell[...] + BS * (lax.broadcasted_iota(jnp.int32, (rows, 1), 0) // per)
    hot = lax.broadcasted_iota(jnp.int32, shape, 1) == place
    observed = dot1(hot.astype(F32).astype(BF16), stacked, 1, 0).astype(BF16)
    predicted = jnp.sum(jnp.where(hot, mean, 0.0), axis=1, keepdims=True)
    pull = weight[...] * (level[...] - predicted)
    return stacked, mean, observed, pull


def add_gram(gram, left, rights, fresh):
    count = left.shape[1] // BS
    at = 0
    for i in range(count):
        part = sum(dot1(left[:, BS * i : BS * i + BS], r[:, BS * i :], 0, 0) for r in rights)
        for j in range(count - i):
            rows = pl.ds(BS * at, BS)
            block = part[:, BS * j : BS * j + BS]
            gram[rows, :] = block if fresh else gram[rows, :] + block
            at += 1


def inner_kernel(index_ref, source, mean_source, tiles, noise, cell, level, weight, out, mean_out, seen, pull, gram):
    step = pl.program_id(0)

    @pl.when(step == 0)
    def _():
        gram[...] = jnp.zeros_like(gram)

    stacked, mean, observed, force = forecast_step(
        step, index_ref, source, mean_source, tiles, noise, cell, level, weight
    )
    out[...] = stacked
    mean_out[0] = mean
    seen[...] = observed
    pull[...] = force
    add_gram(gram, stacked, [stacked], False)


def outer_kernel(
    index_ref, before, low, high, after, mean_source, tiles, noise, cell, level, weight, weights, seen_in, pull_in,
    gram_in, unused, out, mean_out, payload, source, seen, pull,
):
    step = pl.program_id(0)
    count = low.shape[0]
    inner = seen_in.shape[0]
    rows = cell.shape[0]
    grams = gram_in.shape[0]

    @pl.when(step == 0)
    def _():
        source[0:SPAN] = before[...]
        source[SPAN : SPAN + count] = low[...]
        source[SPAN + count : SPAN + 2 * count] = high[...]
        source[SPAN + 2 * count :] = after[...]
        seen[0:inner] = seen_in[...]
        pull[0:inner] = pull_in[...]
        payload[0:grams, :] = gram_in[...]

    stacked, mean, observed, force = forecast_step(
        step, index_ref, source, mean_source, tiles, noise, cell, level, weight
    )
    out[...] = stacked
    mean_out[0] = mean
    here = pl.ds(pl.multiple_of(inner + step * rows, 16), rows)
    seen[here, :] = observed
    pull[here, :] = force
    add_gram(payload, stacked, [stacked], False)

    @pl.when(step == pl.num_programs(0) - 1)
    def _():
        rows_seen = seen[...]
        weighted = split(rows_seen.astype(F32) * weights[...])
        add_gram(payload.at[pl.ds(grams, grams), :], rows_seen, weighted, True)
        force = pull[...]
        first, rest = split(force)
        second, third = split(force - first.astype(F32))
        lane = lax.broadcasted_iota(jnp.int32, (force.shape[0], BS), 1)
        parts = jnp.where(lane == 0, first.astype(F32), 0.0)
        parts = jnp.where(lane == 1, second.astype(F32), parts)
        parts = jnp.where(lane == 2, third.astype(F32), parts).astype(BF16)
        line = jnp.sum(dot1(parts, rows_seen, 0, 0)[0:8], axis=0, keepdims=True)
        payload[2 * grams :, :] = jnp.zeros((payload.shape[0] - 2 * grams, BS), F32)
        for i in range(line.shape[1] // BS):
            payload[2 * grams + i : 2 * grams + i + 1, :] = line[:, BS * i : BS * i + BS]


def factor(groups):
    sub = lax.broadcasted_iota(jnp.int32, (8, 128), 0)
    spread = lambda v: jnp.broadcast_to(v, (8, 128))
    groups = list(groups)
    for p in range(len(groups)):
        columns = [spread(groups[p][:, 8 * p + j : 8 * p + j + 1]) for j in range(8)]
        x = groups[p]
        entries, scales, rows = [], [], []
        for j in range(8):
            scale = lax.rsqrt(spread(columns[j][j : j + 1, :]))
            column = columns[j] * scale
            entry = {}
            for m in range(j + 1, 8):
                entry[m] = spread(column[m : m + 1, :])
                columns[m] = columns[m] - column * entry[m]
            row = spread(x[j : j + 1, :]) * scale
            x = jnp.where(sub == j, row, x - jnp.where(sub > j, column, 0.0) * row)
            entries.append(entry)
            scales.append(scale)
            rows.append(row)
        groups[p] = x
        for g in range(p + 1, len(groups)):
            columns = [spread(groups[g][:, 8 * p + j : 8 * p + j + 1]) for j in range(8)]
            total = groups[g]
            for j in range(8):
                column = columns[j] * scales[j]
                for m in range(j + 1, 8):
                    columns[m] = columns[m] - column * entries[j][m]
                total = total - column * rows[j]
            groups[g] = total
    return groups


def eliminate(work, out, n):
    eye = lax.broadcasted_iota(jnp.int32, (NB, 128 - NB), 0) == lax.broadcasted_iota(jnp.int32, (NB, 128 - NB), 1)
    eye = eye.astype(F32)
    for s in range(n // NB):
        top = s * NB
        block = jnp.concatenate([work[top : top + NB, top : top + NB], eye], axis=1)
        done = factor([block[8 * g : 8 * g + 8, :] for g in range(NB // 8)])
        inverse = jnp.concatenate(done, axis=0)[:, NB : 2 * NB]
        start = (top + NB) // 128 * 128
        row = dot3(split(inverse), split(work[top : top + NB, start:]), 1, 0)
        out[top : top + NB, :] = row[:, n - start :]
        row = split(row)
        for t in range(s + 1, n // NB):
            at = t * NB
            first = at // 128 * 128
            left = tuple(r[:, at - start : at - start + NB] for r in row)
            right = tuple(r[:, first - start :] for r in row)
            work[at : at + NB, first:] = work[at : at + NB, first:] - dot3(left, right, 0, 0)


def diagonal(block):
    shape = (BS, BS)
    same = lax.broadcasted_iota(jnp.int32, shape, 0) == lax.broadcasted_iota(jnp.int32, shape, 1)
    return jnp.sum(jnp.where(same, block, 0.0), axis=1, keepdims=True)


def precondition_kernel(payload, basis, out, work):
    cols, n = basis.shape
    count = cols // BS
    at = [pairs(count).index((i, i)) for i in range(count)]
    size = jnp.concatenate([diagonal(payload[BS * a : BS * a + BS, :]) for a in at], axis=0)
    top = jnp.max(size)
    size = jnp.where(top > 0, jnp.maximum(size * (1 / jnp.where(top > 0, top, 1.0)), 1 / 32), 1.0)
    start = basis[...].astype(F32)
    scaled = (start * size).astype(BF16)
    work[:, :n] = dot1(scaled, scaled, 0, 0)
    work[:, n:] = start.T
    eliminate(work, out, n)


def analysis_kernel(place_ref, chunks, begin, factor_out, shift_out, work, whole, gram, info):
    n, cols = begin.shape
    count = cols // BS
    number, rows, _ = chunks.shape
    for c in range(number):
        whole[rows * c : rows * c + rows, :] = chunks[place_ref[c]]
    listed = pairs(count)
    grams = BS * len(listed)
    top = functools.reduce(
        jnp.maximum, [jnp.max(diagonal(whole[BS * listed.index((i, i)) : BS * listed.index((i, i)) + BS, :])) for i in range(count)]
    )
    scale = 1 / top
    for a, (i, j) in enumerate(listed):
        for target, first, factor_of in ((gram, 0, scale), (info, grams, 1.0)):
            block = whole[first + BS * a : first + BS * a + BS, :] * factor_of
            target[BS * i : BS * i + BS, BS * j : BS * j + BS] = block
            if i != j:
                target[BS * j : BS * j + BS, BS * i : BS * i + BS] = block.T
    pull = jnp.concatenate([whole[2 * grams + i : 2 * grams + i + 1, :] for i in range(count)], axis=1)
    both = split(gram[...])
    once = dot3(split(begin[...]), both, 1, 0)
    twice = dot3(split(once), both, 1, 0)
    parts = split(twice)
    full = twice + dot3(parts, split(info[...]), 1, 0)
    work[:, :n] = dot3(split(full), parts, 1, 1)
    work[:, n:] = twice
    final = gram.at[0:n, :]
    eliminate(work, final, n)
    result = final[...]
    factor_out[...] = result.astype(BF16)
    parts = split(result)
    pull = split(jnp.broadcast_to(pull, (16, cols)))
    inner = dot3(pull, parts, 1, 1)
    shift = dot3(split(inner), parts, 1, 0)
    first, second = split(shift)
    line = lax.broadcasted_iota(jnp.int32, shift.shape, 0)
    both = jnp.where(line == 0, first.astype(F32), jnp.where(line == 1, second.astype(F32), 0.0))
    shift_out[...] = both.astype(BF16)


def posterior_kernel(stacked, factor_ref, shift, mean, root_out, mean_out):
    rows = stacked[...]
    root_out[...] = dot1(rows, factor_ref[...], 1, 1).astype(BF16)
    change = dot1(shift[...], rows, 1, 1)
    mean_out[0] = mean[0] + jnp.sum(change[0:8], axis=0, keepdims=True)


def stages(count):
    found, stride = [], 1
    while count > 1:
        size = 4 if count % 4 == 0 and stride > 2 else 2 if count % 2 == 0 else count
        found.append((stride, size))
        stride, count = stride * size, count // size
    return found


def moved(x, axis, total, stride, size, step):
    def target(i):
        digit = i // stride % size
        return i + ((digit + step) % size - digit) * stride

    return lax.ppermute(x, axis, [(i, target(i)) for i in range(total)])


def summed(x, axis):
    total = lax.axis_size(axis)
    me = lax.axis_index(axis)
    levels = stages(total)
    for stride, size in levels:
        digit = me // stride % size
        part = x.shape[0] // size
        pick = lambda d: lax.dynamic_slice_in_dim(x, d % size * part, part, axis=0)
        got = [moved(pick(digit + k), axis, total, stride, size, k) for k in range(1, size)]
        x = functools.reduce(jnp.add, got, pick(digit))
    rows = x.shape[0]
    place = jnp.zeros((), jnp.int32)
    chunk = jnp.arange(total)
    weight = 1
    for stride, size in reversed(levels):
        x = jnp.concatenate([x] + [moved(x, axis, total, stride, size, k) for k in range(1, size)], axis=0)
        digit = me // stride % size
        place = place + (digit - chunk // (total // (stride * size)) % size) % size * weight
        weight *= size
    return x.reshape(total, rows, x.shape[1]), place.astype(jnp.int32)


def local(
    prior_mean,
    prior_root,
    process_noise_factor,
    tangent_operator_tiles,
    tile_target_placing,
    start_basis,
    obs_cell,
    measured_surge_levels,
    obs_precision,
):
    blocks = tile_target_placing.shape[0]
    rank = prior_root.shape[1]
    noise = process_noise_factor.shape[1]
    cols = rank + noise
    nobs = obs_cell.shape[1]
    total = lax.axis_size("state")
    ends = total - 1
    inner = blocks - 2 * SPAN
    near = 2 * SPAN

    tail = prior_root[-SPAN * BS :]
    head = prior_root[: SPAN * BS]
    up = [(i, i + 1) for i in range(ends)]
    down = [(i + 1, i) for i in range(ends)]
    mean = prior_mean.astype(F32).reshape(blocks, BS)
    before = lax.ppermute(tail, "state", up).reshape(SPAN, BS, rank)
    after = lax.ppermute(head, "state", down).reshape(SPAN, BS, rank)
    mean_before = lax.ppermute(prior_mean[-SPAN * BS :], "state", up).astype(F32).reshape(SPAN, BS)
    mean_after = lax.ppermute(prior_mean[: SPAN * BS], "state", down).astype(F32).reshape(SPAN, BS)
    mean_near = jnp.concatenate([mean_before, mean[:near], mean[-near:], mean_after], axis=0)

    relative = tile_target_placing - lax.axis_index("state") * blocks
    inner_index = relative[SPAN:-SPAN].reshape(-1)
    outer_index = jnp.concatenate(
        [relative[:SPAN] + SPAN, relative[-SPAN:] - (blocks - near) + SPAN + near], axis=0
    ).reshape(-1)

    def column(x):
        ordered = jnp.concatenate([x[SPAN:-SPAN], x[:SPAN], x[-SPAN:]], axis=0)
        return ordered.reshape(-1, 1)

    cell, level, weight = column(obs_cell), column(measured_surge_levels), column(obs_precision)
    source = prior_root.reshape(blocks, BS, rank)
    grams = BS * len(pairs(cols // BS))
    rows = GROUP * BS
    seen_rows = GROUP * nobs
    steps = inner // GROUP
    at_one = lambda i, *_: (i, 0)

    stacked, mean_inner, seen, pull, gram = pl.pallas_call(
        inner_kernel,
        out_shape=(
            jax.ShapeDtypeStruct((blocks * BS, cols), BF16),
            jax.ShapeDtypeStruct((steps, 1, rows), F32),
            jax.ShapeDtypeStruct((inner * nobs, cols), BF16),
            jax.ShapeDtypeStruct((inner * nobs, 1), F32),
            jax.ShapeDtypeStruct((grams, BS), F32),
        ),
        grid_spec=pltpu.PrefetchScalarGridSpec(
            num_scalar_prefetch=1,
            grid=(steps,),
            in_specs=[
                pl.BlockSpec((blocks, BS, rank), lambda i, *_: (0, 0, 0), pipeline_mode=pl.Buffered(1)),
                pl.BlockSpec((blocks, BS), lambda i, *_: (0, 0)),
                pl.BlockSpec((GROUP, 3, BS, BS), lambda i, *_: (i + SPAN // GROUP, 0, 0, 0)),
                pl.BlockSpec((rows, noise), lambda i, *_: (i + SPAN // GROUP, 0)),
                pl.BlockSpec((seen_rows, 1), at_one),
                pl.BlockSpec((seen_rows, 1), at_one),
                pl.BlockSpec((seen_rows, 1), at_one),
            ],
            out_specs=[
                pl.BlockSpec((rows, cols), lambda i, *_: (i + SPAN // GROUP, 0)),
                pl.BlockSpec((1, 1, rows), lambda i, *_: (i, 0, 0)),
                pl.BlockSpec((seen_rows, cols), at_one),
                pl.BlockSpec((seen_rows, 1), at_one),
                pl.BlockSpec((grams, BS), lambda i, *_: (0, 0)),
            ],
        ),
        compiler_params=LIMIT,
        name="forecast_inner",
    )(inner_index, source, mean, tangent_operator_tiles, process_noise_factor, cell, level, weight)

    end_steps = 2 * SPAN // GROUP
    unit = 8 * total
    payload_rows = -(-(2 * grams + cols // BS) // unit) * unit
    end = lambda i: jnp.where(i < SPAN // GROUP, i, blocks // GROUP - end_steps + i)
    first = inner // GROUP
    stacked, mean_outer, payload = pl.pallas_call(
        outer_kernel,
        out_shape=(
            jax.ShapeDtypeStruct((blocks * BS, cols), BF16),
            jax.ShapeDtypeStruct((end_steps, 1, rows), F32),
            jax.ShapeDtypeStruct((payload_rows, BS), F32),
        ),
        grid_spec=pltpu.PrefetchScalarGridSpec(
            num_scalar_prefetch=1,
            grid=(end_steps,),
            in_specs=[
                pl.BlockSpec((SPAN, BS, rank), lambda i, *_: (0, 0, 0)),
                pl.BlockSpec((near, BS, rank), lambda i, *_: (0, 0, 0)),
                pl.BlockSpec((near, BS, rank), lambda i, *_: (blocks // near - 1, 0, 0)),
                pl.BlockSpec((SPAN, BS, rank), lambda i, *_: (0, 0, 0)),
                pl.BlockSpec(mean_near.shape, lambda i, *_: (0, 0)),
                pl.BlockSpec((GROUP, 3, BS, BS), lambda i, *_: (end(i), 0, 0, 0)),
                pl.BlockSpec((rows, noise), lambda i, *_: (end(i), 0)),
                pl.BlockSpec((seen_rows, 1), lambda i, *_: (first + i, 0)),
                pl.BlockSpec((seen_rows, 1), lambda i, *_: (first + i, 0)),
                pl.BlockSpec((seen_rows, 1), lambda i, *_: (first + i, 0)),
                pl.BlockSpec(weight.shape, lambda i, *_: (0, 0)),
                pl.BlockSpec(seen.shape, lambda i, *_: (0, 0)),
                pl.BlockSpec(pull.shape, lambda i, *_: (0, 0)),
                pl.BlockSpec(gram.shape, lambda i, *_: (0, 0)),
                pl.BlockSpec(memory_space=pl.ANY),
            ],
            out_specs=[
                pl.BlockSpec((rows, cols), lambda i, *_: (end(i), 0)),
                pl.BlockSpec((1, 1, rows), lambda i, *_: (i, 0, 0)),
                pl.BlockSpec((payload_rows, BS), lambda i, *_: (0, 0)),
            ],
            scratch_shapes=[
                VMEM((2 * (SPAN + near), BS, rank), BF16),
                VMEM((blocks * nobs, cols), BF16),
                VMEM((blocks * nobs, 1), F32),
            ],
        ),
        input_output_aliases={15: 0},
        compiler_params=LIMIT,
        name="forecast_outer",
    )(
        outer_index, before, source, source, after, mean_near, tangent_operator_tiles, process_noise_factor,
        cell, level, weight, weight, seen, pull, gram, stacked,
    )
    mean_lines = jnp.concatenate([mean_outer[: SPAN // GROUP], mean_inner, mean_outer[SPAN // GROUP :]], axis=0)

    begin = pl.pallas_call(
        precondition_kernel,
        out_shape=jax.ShapeDtypeStruct((rank, cols), F32),
        in_specs=[pl.BlockSpec(memory_space=VMEM)] * 2,
        out_specs=pl.BlockSpec(memory_space=VMEM),
        scratch_shapes=[VMEM((rank, rank + cols), F32)],
        compiler_params=LIMIT,
        name="precondition",
    )(payload[:grams], start_basis)

    chunks, place = summed(payload, "state")

    factor_t, shift = pl.pallas_call(
        analysis_kernel,
        out_shape=(jax.ShapeDtypeStruct((rank, cols), BF16), jax.ShapeDtypeStruct((16, cols), BF16)),
        grid_spec=pltpu.PrefetchScalarGridSpec(
            num_scalar_prefetch=1,
            grid=(1,),
            in_specs=[
                pl.BlockSpec(chunks.shape, lambda i, *_: (0, 0, 0)),
                pl.BlockSpec(begin.shape, lambda i, *_: (0, 0)),
            ],
            out_specs=[
                pl.BlockSpec((rank, cols), lambda i, *_: (0, 0)),
                pl.BlockSpec((16, cols), lambda i, *_: (0, 0)),
            ],
            scratch_shapes=[
                VMEM((rank, rank + cols), F32),
                VMEM((payload_rows, BS), F32),
                VMEM((cols, cols), F32),
                VMEM((cols, cols), F32),
            ],
        ),
        compiler_params=LIMIT,
        name="analysis",
    )(place, chunks, begin)

    tile = 4 * BS
    tiles = blocks * BS // tile
    posterior_root, posterior_mean = pl.pallas_call(
        posterior_kernel,
        out_shape=(
            jax.ShapeDtypeStruct((blocks * BS, rank), BF16),
            jax.ShapeDtypeStruct((tiles, 1, tile), F32),
        ),
        grid=(tiles,),
        in_specs=[
            pl.BlockSpec((tile, cols), lambda i: (i, 0)),
            pl.BlockSpec((rank, cols), lambda i: (0, 0)),
            pl.BlockSpec((16, cols), lambda i: (0, 0)),
            pl.BlockSpec((1, 1, tile), lambda i: (i, 0, 0)),
        ],
        out_specs=[
            pl.BlockSpec((tile, rank), lambda i: (i, 0)),
            pl.BlockSpec((1, 1, tile), lambda i: (i, 0, 0)),
        ],
        compiler_params=LIMIT,
        name="posterior",
    )(stacked, factor_t, shift, mean_lines.reshape(tiles, 1, tile))
    return (posterior_mean.reshape(-1), posterior_root)


def solution(mesh):
    placed = (
        P(("grp", "state")),
        P(("grp", "state"), None),
        P(("grp", "state"), None),
        P(("grp", "state"), None, None, None),
        P(("grp", "state"), None),
        P(),
        P(("grp", "state"), None),
        P(("grp", "state"), None),
        P(("grp", "state"), None),
    )
    return jax.shard_map(
        local,
        mesh=mesh,
        in_specs=placed,
        out_specs=(P(("grp", "state")), P(("grp", "state"), None)),
        check_vma=False,
    )
```
